32 devices in a mesh: freq: 8 (over z, x), bl: 4 (over y, core).
Axes of the slice: x: 2, y: 2, z: 4, core: 2. Of those that a mesh axis runs over, the one named last changes fastest.
Arguments:
- voltages: bfloat16 [1024, 134144], P(('bl', 'freq')), may hold values from -6 to 6
- fir_taps: float32 [4, 1024], replicated, may hold values from -3 to 3
- antenna_order: int32 [1024], replicated, may hold values from 0 to 1023, each once
- tile_list: int32 [4, 2], replicated, may hold values from 0 to 3
Outputs:
- visibilities: bfloat16 [4, 512, 256, 512], P('bl', 'freq')
The draws below stay inside these ranges and needn't reach their ends.
All inputs are finite; a program needn't handle non-finite values.
Results may differ from the reference program's by a relative error of at most 0.0074.
Values may be sent and summed in bfloat16 or wider, within the bound.
A program may use at most 128 MiB of HBM per device.

```python
import math
import jax
import jax.numpy as jnp
from jax import lax

A = 1024
K = 1024
TAPS = 4
PANEL = 256
SAMPLES = 128
CHANNELS = 512
PANELS = 4
SPAN = 134144
N_BL = 4


def plant(array, rng, low, high):
    shape = array.shape
    index_at = [jax.random.randint(jax.random.fold_in(rng, axis), (), 0, shape[axis]) for axis in range(len(shape))]
    array = array.at[tuple(index_at)].set(low)
    longest = shape.index(max(shape))
    index_at[longest] = (index_at[longest] + 1) % shape[longest]
    return array.at[tuple(index_at)].set(high)


def shard_levels(rng, extent, cuts, least, largest):
    gain, own = 1.0, jax.random.fold_in(rng, 6)
    for axis_at, parts in cuts:
        heights = jnp.exp(jax.random.uniform(jax.random.fold_in(own, axis_at), (parts,), jnp.float32, least / len(cuts), largest / len(cuts)))
        gain = gain * jnp.repeat(heights, extent[axis_at] // parts).reshape([-1 if axis == axis_at else 1 for axis in range(len(extent))])
    return gain


def centred(stream_key, dims, scale, most, pieces=(), kind=jnp.bfloat16):
    loudness = shard_levels(stream_key, dims, pieces, -0.22, 0.18) if pieces else 1.0
    entries = jax.random.normal(stream_key, dims, jnp.float32) * scale * loudness
    return jnp.minimum(jnp.maximum(entries, -most), most).astype(kind)


def setup_inputs(seed: int = 0) -> dict:
    keys = jax.random.split(jax.random.key(seed), 5)
    return {
        "voltages": centred(keys[0], (A, SPAN), 1.0, 6.0, ((0, 32),)),
        "fir_taps": centred(keys[1], (TAPS, K), TAPS ** -0.5, 3.0, (), jnp.float32),
        "antenna_order": jax.random.permutation(keys[2], A).astype(jnp.int32),
        "tile_list": plant(jax.random.randint(keys[3], (N_BL, 2), 0, PANELS), jax.random.fold_in(keys[3], 1), 0, PANELS - 1).astype(jnp.int32),
    }


def make_table(points, kept):
    product = jnp.arange(points, dtype=jnp.int32)[:, None] * jnp.arange(kept, dtype=jnp.int32)[None, :] % points
    phase = 2.0 * math.pi / points * product.astype(jnp.float32)
    return jnp.concatenate([jnp.cos(phase), -jnp.sin(phase)], axis=1).astype(jnp.bfloat16)

def arrange(panel):
    width = panel.shape[1]
    return jnp.transpose(panel, (3, 0, 2, 1)).reshape(panel.shape[3], panel.shape[0], 2 * width)

def rotated(panel):
    turned = jnp.stack([-panel[:, :, 1, :], panel[:, :, 0, :]], axis=2)
    return arrange(turned)

def reference(voltages, fir_taps, antenna_order, tile_list):
    frames = voltages.reshape(A, SAMPLES + TAPS - 1, K).astype(jnp.float32)
    filtered = jnp.zeros((A, SAMPLES, K), jnp.float32)
    for tap in range(TAPS):
        filtered = filtered + fir_taps[tap][None, None, :] * frames[:, tap:tap + SAMPLES, :]
    filtered = filtered.astype(jnp.bfloat16)
    table = make_table(K, CHANNELS)
    spectra = jnp.dot(filtered.reshape(A * SAMPLES, K), table, preferred_element_type=jnp.float32)
    spectra = (spectra * (1.0 / math.sqrt(K))).astype(jnp.bfloat16).reshape(A, SAMPLES, 2, CHANNELS)

    def one_tile(tile):
        row_ids = lax.dynamic_slice_in_dim(antenna_order, (tile[0] * PANEL).astype(jnp.int32), PANEL)
        col_ids = lax.dynamic_slice_in_dim(antenna_order, (tile[1] * PANEL).astype(jnp.int32), PANEL)
        row_panel = jnp.take(spectra, row_ids, axis=0)
        col_panel = jnp.take(spectra, col_ids, axis=0)
        left = arrange(row_panel).astype(jnp.float32)
        right = jnp.concatenate([arrange(col_panel), rotated(col_panel)], axis=1).astype(jnp.float32)
        summed = jnp.einsum('fps,fqs->fpq', left, right)
        return (summed / SAMPLES).astype(jnp.bfloat16)
    return lax.map(one_tile, tile_list)
```

```python
import functools
import math

import jax
import jax.numpy as jnp
import numpy as np
from jax import lax
from jax.experimental import pallas as pl
from jax.experimental.pallas import tpu as pltpu
from jax.sharding import PartitionSpec as P

K = 1024
TAPS = 4
PANEL = 256
SAMPLES = 128
LANES = 128
WIDE = 16
NARROW = 8
MESH = pl.DeviceIdType.MESH


def make_table(points, kept):
    product = (
        jnp.arange(points, dtype=jnp.int32)[:, None]
        * jnp.arange(kept, dtype=jnp.int32)[None, :]
        % points
    )
    phase = 2.0 * math.pi / points * product.astype(jnp.float32)
    return jnp.concatenate([jnp.cos(phase), -jnp.sin(phase)], axis=1).astype(jnp.bfloat16)


def arrange(panel):
    width = panel.shape[1]
    return jnp.transpose(panel, (3, 0, 2, 1)).reshape(panel.shape[3], panel.shape[0], 2 * width)


def rotated(panel):
    turned = jnp.stack([-panel[:, :, 1, :], panel[:, :, 0, :]], axis=2)
    return arrange(turned)


def picked(source, ids):
    pick = (ids[:, None] == jnp.arange(source.shape[0], dtype=jnp.int32)[None, :]).astype(jnp.bfloat16)
    return jnp.einsum("at,tspf->aspf", pick, source, preferred_element_type=jnp.float32).astype(jnp.bfloat16)


def correlate(source, antenna_order, tile):
    row_ids = lax.dynamic_slice_in_dim(antenna_order, tile[0] * PANEL, PANEL)
    col_ids = lax.dynamic_slice_in_dim(antenna_order, tile[1] * PANEL, PANEL)
    row_panel = picked(source, row_ids)
    col_panel = picked(source, col_ids)
    left = arrange(row_panel)
    right = jnp.concatenate([arrange(col_panel), rotated(col_panel)], axis=1)
    return jnp.einsum("fps,fqs->fpq", left, right, preferred_element_type=jnp.float32)


def per_device_plain(voltages, fir_taps, antenna_order, tile_list):
    local_count = voltages.shape[0]
    frames = voltages.reshape(local_count, SAMPLES + TAPS - 1, K)
    filtered = jnp.zeros((local_count, SAMPLES, K), jnp.float32)
    for tap in range(TAPS):
        filtered = filtered + fir_taps[tap][None, None, :] * frames[
            :, tap : tap + SAMPLES, :
        ].astype(jnp.float32)
    filtered = filtered.astype(jnp.bfloat16)
    table = make_table(K, K // 2)
    spectra = jnp.dot(
        filtered.reshape(local_count * SAMPLES, K), table, preferred_element_type=jnp.float32
    )
    spectra = (
        (spectra * (1.0 / math.sqrt(K)))
        .astype(jnp.bfloat16)
        .reshape(local_count, SAMPLES, 2, K // 2)
    )
    turned = lax.all_to_all(spectra, "freq", split_axis=3, concat_axis=0, tiled=True)
    gathered = lax.all_gather(turned, "bl", axis=0, tiled=True)
    own_tile = tile_list[lax.axis_index("bl")]
    summed = correlate(gathered, antenna_order, own_tile)
    return (summed / SAMPLES).astype(jnp.bfloat16)[None]


def chunked_table(groups, width):
    m = np.arange(K)[None, :] * np.arange(K // 2)[:, None] % K
    phase = 2.0 * math.pi / K * m
    table = np.stack([np.cos(phase), -np.sin(phase)])
    table = table.reshape(2, groups, -1, width, K).transpose(2, 0, 1, 3, 4)
    return table.reshape(table.shape[0], 2 * groups * width, K).astype(jnp.bfloat16)


def spectra_kernel(
    groups, tiles, volt_ref, taps_ref, table_ref, all_ref,
    filt32, filt, turn, send, own_sem, s1, r1, s2, r2, s3, r3, s4, r4,
):
    me = lax.axis_index("freq")
    bl = lax.axis_index("bl")
    core = bl % 2
    mate = bl + 1 - 2 * core
    across = [(bl + 2 * e) % tiles for e in range(1, tiles // 2)]
    ants = volt_ref.shape[0]
    block = groups * ants

    barrier = pltpu.get_barrier_semaphore()
    for d in range(1, groups):
        pl.semaphore_signal(barrier, inc=1, device_id={"freq": (me + d) % groups}, device_id_type=MESH)
    for there in (mate, *across):
        pl.semaphore_signal(barrier, inc=1, device_id={"bl": there}, device_id_type=MESH)
    pl.semaphore_wait(barrier, groups - 1 + 1 + len(across))

    @pl.loop(0, SAMPLES // 8)
    def _(step):
        for half in range(K // 256):
            cols = 256 * half
            taps = [taps_ref[t : t + 1, cols : cols + 256] for t in range(TAPS)]
            frames = []
            for i in range(8 + TAPS - 1):
                at = pl.multiple_of((step * 8 + i) * K, K) + cols
                frames.append(volt_ref[:, pl.ds(pl.multiple_of(at, 256), 256)].astype(jnp.float32))
            for i in range(8):
                total = taps[0] * frames[i]
                for t in range(1, TAPS):
                    total = total + taps[t] * frames[i + t]
                for q in range(2):
                    filt32[2 * half + q, pl.ds(step * 8 + i, ants, stride=SAMPLES), :] = total[
                        :, q * LANES : (q + 1) * LANES
                    ]

    @pl.loop(0, ants)
    def _(a):
        rows = pl.ds(pl.multiple_of(a * SAMPLES, SAMPLES), SAMPLES)
        for q in range(K // LANES):
            filt[rows, q * LANES : (q + 1) * LANES] = filt32[q, rows, :].astype(jnp.bfloat16)

    steps = table_ref.shape[0]
    per = WIDE // NARROW
    rows_of = groups * WIDE

    def turn_copies(c):
        h, w = c % per, c // per
        copies = []
        for d in range(1, groups):
            to = (me + d) % groups
            copies.append(
                pltpu.make_async_remote_copy(
                    src_ref=send.at[w, pl.ds(to * WIDE + h * NARROW, NARROW)],
                    dst_ref=all_ref.at[
                        pl.ds(c * NARROW, NARROW), pl.ds(pl.multiple_of(bl * block + me * ants, ants), ants)
                    ],
                    send_sem=s1.at[c, d],
                    recv_sem=r1.at[c, d],
                    device_id={"freq": to},
                    device_id_type=MESH,
                )
            )
        own = pltpu.make_async_copy(
            send.at[w, pl.ds(me * WIDE + h * NARROW, NARROW)],
            all_ref.at[pl.ds(c * NARROW, NARROW), pl.ds(pl.multiple_of(bl * block + me * ants, ants), ants)],
            own_sem.at[c],
        )
        return copies, own

    def block_of(c, b):
        return all_ref.at[pl.ds(c * NARROW, NARROW), pl.ds(pl.multiple_of(b * block, block), block)]

    def block_copy(c, b, there, ssem, rsem):
        return pltpu.make_async_remote_copy(
            src_ref=block_of(c, b), dst_ref=block_of(c, b), send_sem=ssem, recv_sem=rsem,
            device_id={"bl": there}, device_id_type=MESH,
        )

    def across_copies(c):
        return [block_copy(c, bl, there, s2.at[c, e], r2.at[c, e]) for e, there in enumerate(across)]

    def mate_copy(c):
        return block_copy(c, bl, mate, s3.at[c], r3.at[c])

    def passed_copies(c):
        return [
            block_copy(c, (bl + tiles - 2 * (e + 1)) % tiles, mate, s4.at[c, e], r4.at[c, e])
            for e in range(len(across))
        ]

    chunks = steps * per

    def spread(c):
        copies, own = turn_copies(c)
        for copy in copies:
            copy.wait_recv()
        own.wait()
        for copy in across_copies(c):
            copy.start()
        mate_copy(c).start()

    def hand_on(c):
        arrived, passed = across_copies(c), passed_copies(c)
        for one, two in zip(arrived, passed):
            one.wait_recv()
            two.start()

    for w in range(steps):

        @pl.loop(0, ants // 4)
        def _(q):
            rows = pl.ds(pl.multiple_of(q * 4 * SAMPLES, 4 * SAMPLES), 4 * SAMPLES)
            made = lax.dot_general(
                table_ref[w], filt[rows, :], (((1,), (1,)), ((), ())), preferred_element_type=jnp.float32
            ) * (1.0 / math.sqrt(K))
            for i in range(4):
                for p in range(2):
                    turn[p, pl.ds(q * 4 + i, rows_of, stride=ants), :] = made[
                        p * rows_of : (p + 1) * rows_of, i * SAMPLES : (i + 1) * SAMPLES
                    ]

        @pl.loop(0, rows_of // 8)
        def _(r):
            for p in range(2):
                rows = turn[p, pl.ds(pl.multiple_of(r * 8 * ants, 8 * ants), 8 * ants), :]
                send[w, pl.ds(pl.multiple_of(r * 8, 8), 8), :, p * LANES : (p + 1) * LANES] = rows.reshape(
                    8, ants, LANES
                ).astype(jnp.bfloat16)

        for c in range(w * per, (w + 1) * per):
            if c >= 2:
                for copy in turn_copies(c - 2)[0]:
                    copy.wait_send()
            copies, own = turn_copies(c)
            own.start()
            for copy in copies:
                copy.start()
            if c >= 2:
                spread(c - 2)
            if c >= 4:
                hand_on(c - 4)
    for c in range(chunks - 2, chunks):
        spread(c)
    for c in range(chunks - 4, chunks):
        hand_on(c)
    for c in range(chunks):
        mate_copy(c).wait()
        for copy in across_copies(c):
            copy.wait_send()
        for copy in passed_copies(c):
            copy.wait()
    for c in range(chunks - 2, chunks):
        for copy in turn_copies(c)[0]:
            copy.wait_send()


def correlate_kernel(pick_ref, all_ref, out_ref):
    for f in range(all_ref.shape[0]):
        both = jnp.dot(pick_ref[...], all_ref[f], preferred_element_type=jnp.float32).astype(jnp.bfloat16)
        left, right = both[:PANEL], both[PANEL:]
        turned = jnp.concatenate([-right[:, SAMPLES:], right[:, :SAMPLES]], axis=1)
        for at, other in enumerate((right, turned)):
            summed = lax.dot_general(left, other, (((1,), (1,)), ((), ())), preferred_element_type=jnp.float32)
            out_ref[f, :, at * PANEL : (at + 1) * PANEL] = (summed * (1.0 / SAMPLES)).astype(jnp.bfloat16)


def per_device(groups, tiles, voltages, fir_taps, antenna_order, tile_list):
    ants = voltages.shape[0]
    total = ants * groups * tiles
    channels = K // 2 // groups
    table = jnp.asarray(chunked_table(groups, WIDE))
    steps = channels // WIDE
    chunks = channels // NARROW
    others = max(tiles // 2 - 1, 1)
    dma = pltpu.SemaphoreType.DMA
    gathered = pl.pallas_call(
        functools.partial(spectra_kernel, groups, tiles),
        out_shape=jax.ShapeDtypeStruct((channels, total, 2 * SAMPLES), jnp.bfloat16),
        in_specs=[pl.BlockSpec(memory_space=pltpu.VMEM)] * 3,
        out_specs=pl.BlockSpec(memory_space=pl.ANY),
        scratch_shapes=[
            pltpu.VMEM((K // LANES, ants * SAMPLES, LANES), jnp.float32),
            pltpu.VMEM((ants * SAMPLES, K), jnp.bfloat16),
            pltpu.VMEM((2, groups * WIDE * ants, LANES), jnp.float32),
            pltpu.VMEM((steps, groups * WIDE, ants, 2 * SAMPLES), jnp.bfloat16),
            dma((chunks,)),
            dma((chunks, groups)), dma((chunks, groups)),
            dma((chunks, others)), dma((chunks, others)),
            dma((chunks,)), dma((chunks,)),
            dma((chunks, others)), dma((chunks, others)),
        ],
        cost_estimate=pl.CostEstimate(flops=10**10, bytes_accessed=10**8, transcendentals=0),
        compiler_params=pltpu.CompilerParams(
            collective_id=0, has_side_effects=True, vmem_limit_bytes=58 * 2**20
        ),
        name="spectra",
    )(voltages, fir_taps, table)

    tile = tile_list[lax.axis_index("bl")]
    ids = jnp.concatenate(
        [lax.dynamic_slice_in_dim(antenna_order, tile[i] * PANEL, PANEL) for i in range(2)]
    )
    pick = (ids[:, None] == jnp.arange(total, dtype=jnp.int32)[None, :]).astype(jnp.bfloat16)
    at_once = 4
    seen = pl.pallas_call(
        correlate_kernel,
        grid=(channels // at_once,),
        out_shape=jax.ShapeDtypeStruct((channels, PANEL, 2 * PANEL), jnp.bfloat16),
        in_specs=[
            pl.BlockSpec((2 * PANEL, total), lambda i: (0, 0)),
            pl.BlockSpec((at_once, total, 2 * SAMPLES), lambda i: (i, 0, 0)),
        ],
        out_specs=pl.BlockSpec((at_once, PANEL, 2 * PANEL), lambda i: (i, 0, 0)),
        compiler_params=pltpu.CompilerParams(vmem_limit_bytes=32 * 2**20),
        name="correlate",
    )(pick, gathered)
    return seen[None]


def solution(mesh):
    groups, tiles = mesh.shape["freq"], mesh.shape["bl"]

    def run(voltages, fir_taps, antenna_order, tile_list):
        if voltages.shape[0] % 16 == 0 and (K // 2 // groups) % WIDE == 0 and tiles % 2 == 0:
            body = functools.partial(per_device, groups, tiles)
        else:
            body = per_device_plain
        return body(voltages, fir_taps, antenna_order, tile_list)

    return jax.shard_map(
        run,
        mesh=mesh,
        in_specs=(P(("bl", "freq"), None), P(), P(), P()),
        out_specs=P("bl", "freq", None, None),
        check_vma=False,
    )
```

```python
import functools
import math

import jax
import jax.numpy as jnp
import numpy as np
from jax import lax
from jax.experimental import pallas as pl
from jax.experimental.pallas import tpu as pltpu
from jax.sharding import PartitionSpec as P

K = 1024
TAPS = 4
PANEL = 256
SAMPLES = 128
LANES = 128
WIDE = 16
NARROW = 4
AHEAD = 3
MESH = pl.DeviceIdType.MESH


def make_table(points, kept):
    product = (
        jnp.arange(points, dtype=jnp.int32)[:, None]
        * jnp.arange(kept, dtype=jnp.int32)[None, :]
        % points
    )
    phase = 2.0 * math.pi / points * product.astype(jnp.float32)
    return jnp.concatenate([jnp.cos(phase), -jnp.sin(phase)], axis=1).astype(jnp.bfloat16)


def arrange(panel):
    width = panel.shape[1]
    return jnp.transpose(panel, (3, 0, 2, 1)).reshape(panel.shape[3], panel.shape[0], 2 * width)


def rotated(panel):
    turned = jnp.stack([-panel[:, :, 1, :], panel[:, :, 0, :]], axis=2)
    return arrange(turned)


def picked(source, ids):
    pick = (ids[:, None] == jnp.arange(source.shape[0], dtype=jnp.int32)[None, :]).astype(jnp.bfloat16)
    return jnp.einsum("at,tspf->aspf", pick, source, preferred_element_type=jnp.float32).astype(jnp.bfloat16)


def correlate(source, antenna_order, tile):
    row_ids = lax.dynamic_slice_in_dim(antenna_order, tile[0] * PANEL, PANEL)
    col_ids = lax.dynamic_slice_in_dim(antenna_order, tile[1] * PANEL, PANEL)
    row_panel = picked(source, row_ids)
    col_panel = picked(source, col_ids)
    left = arrange(row_panel)
    right = jnp.concatenate([arrange(col_panel), rotated(col_panel)], axis=1)
    return jnp.einsum("fps,fqs->fpq", left, right, preferred_element_type=jnp.float32)


def per_device_plain(voltages, fir_taps, antenna_order, tile_list):
    local_count = voltages.shape[0]
    frames = voltages.reshape(local_count, SAMPLES + TAPS - 1, K)
    filtered = jnp.zeros((local_count, SAMPLES, K), jnp.float32)
    for tap in range(TAPS):
        filtered = filtered + fir_taps[tap][None, None, :] * frames[
            :, tap : tap + SAMPLES, :
        ].astype(jnp.float32)
    filtered = filtered.astype(jnp.bfloat16)
    table = make_table(K, K // 2)
    spectra = jnp.dot(
        filtered.reshape(local_count * SAMPLES, K), table, preferred_element_type=jnp.float32
    )
    spectra = (
        (spectra * (1.0 / math.sqrt(K)))
        .astype(jnp.bfloat16)
        .reshape(local_count, SAMPLES, 2, K // 2)
    )
    turned = lax.all_to_all(spectra, "freq", split_axis=3, concat_axis=0, tiled=True)
    gathered = lax.all_gather(turned, "bl", axis=0, tiled=True)
    own_tile = tile_list[lax.axis_index("bl")]
    summed = correlate(gathered, antenna_order, own_tile)
    return (summed / SAMPLES).astype(jnp.bfloat16)[None]


def chunked_table(groups, width):
    m = np.arange(K)[None, :] * np.arange(K // 2)[:, None] % K
    phase = 2.0 * math.pi / K * m
    table = np.stack([np.cos(phase), -np.sin(phase)])
    table = table.reshape(2, groups, -1, width, K).transpose(2, 0, 1, 3, 4)
    return table.reshape(table.shape[0], 2 * groups * width, K).astype(jnp.bfloat16)


def spectra_kernel(
    groups, tiles, volt_ref, taps_ref, table_ref, pick_ref, seen_ref, all_ref,
    filt32, filt, turn, send, held, made_vis, held_sem, seen_sem, own_sem, s1, r1, s2, r2, s3, r3, s4, r4,
):
    me = lax.axis_index("freq")
    bl = lax.axis_index("bl")
    core = bl % 2
    mate = bl + 1 - 2 * core
    across = [(bl + 2 * e) % tiles for e in range(1, tiles // 2)]
    ants = volt_ref.shape[0]
    block = groups * ants

    barrier = pltpu.get_barrier_semaphore()
    for d in range(1, groups):
        pl.semaphore_signal(barrier, inc=1, device_id={"freq": (me + d) % groups}, device_id_type=MESH)
    for there in (mate, *across):
        pl.semaphore_signal(barrier, inc=1, device_id={"bl": there}, device_id_type=MESH)
    pl.semaphore_wait(barrier, groups - 1 + 1 + len(across))

    @pl.loop(0, SAMPLES // 8)
    def _(step):
        for half in range(K // 256):
            cols = 256 * half
            taps = [taps_ref[t : t + 1, cols : cols + 256] for t in range(TAPS)]
            frames = []
            for i in range(8 + TAPS - 1):
                at = pl.multiple_of((step * 8 + i) * K, K) + cols
                frames.append(volt_ref[:, pl.ds(pl.multiple_of(at, 256), 256)].astype(jnp.float32))
            for i in range(8):
                total = taps[0] * frames[i]
                for t in range(1, TAPS):
                    total = total + taps[t] * frames[i + t]
                for q in range(2):
                    filt32[2 * half + q, pl.ds(step * 8 + i, ants, stride=SAMPLES), :] = total[
                        :, q * LANES : (q + 1) * LANES
                    ]

    @pl.loop(0, ants)
    def _(a):
        rows = pl.ds(pl.multiple_of(a * SAMPLES, SAMPLES), SAMPLES)
        for q in range(K // LANES):
            filt[rows, q * LANES : (q + 1) * LANES] = filt32[q, rows, :].astype(jnp.bfloat16)

    steps = table_ref.shape[0]
    per = WIDE // NARROW
    rows_of = groups * WIDE

    def turn_copies(c):
        h, w = c % per, c // per
        copies = []
        for d in range(1, groups):
            to = (me + d) % groups
            copies.append(
                pltpu.make_async_remote_copy(
                    src_ref=send.at[w, pl.ds(to * WIDE + h * NARROW, NARROW)],
                    dst_ref=all_ref.at[
                        pl.ds(c * NARROW, NARROW), pl.ds(pl.multiple_of(bl * block + me * ants, ants), ants)
                    ],
                    send_sem=s1.at[c, d],
                    recv_sem=r1.at[c, d],
                    device_id={"freq": to},
                    device_id_type=MESH,
                )
            )
        own = pltpu.make_async_copy(
            send.at[w, pl.ds(me * WIDE + h * NARROW, NARROW)],
            all_ref.at[pl.ds(c * NARROW, NARROW), pl.ds(pl.multiple_of(bl * block + me * ants, ants), ants)],
            own_sem.at[c],
        )
        return copies, own

    def block_of(c, b):
        return all_ref.at[pl.ds(c * NARROW, NARROW), pl.ds(pl.multiple_of(b * block, block), block)]

    def block_copy(c, b, there, ssem, rsem):
        return pltpu.make_async_remote_copy(
            src_ref=block_of(c, b), dst_ref=block_of(c, b), send_sem=ssem, recv_sem=rsem,
            device_id={"bl": there}, device_id_type=MESH,
        )

    def across_copies(c):
        return [block_copy(c, bl, there, s2.at[c, e], r2.at[c, e]) for e, there in enumerate(across)]

    def mate_copy(c):
        return block_copy(c, bl, mate, s3.at[c], r3.at[c])

    def passed_copies(c):
        return [
            block_copy(c, (bl + tiles - 2 * (e + 1)) % tiles, mate, s4.at[c, e], r4.at[c, e])
            for e in range(len(across))
        ]

    chunks = steps * per

    def spread(c):
        copies, own = turn_copies(c)
        for copy in copies:
            copy.wait_recv()
        own.wait()
        for copy in across_copies(c):
            copy.start()
        mate_copy(c).start()

    def hand_on(c):
        arrived, passed = across_copies(c), passed_copies(c)
        for one, two in zip(arrived, passed):
            one.wait_recv()
            two.start()

    def seen_copy(c):
        return pltpu.make_async_copy(made_vis, seen_ref.at[pl.ds(c * NARROW, NARROW)], seen_sem)

    def products(c):
        mate_copy(c).wait_recv()
        for copy in passed_copies(c):
            copy.wait_recv()
        load = pltpu.make_async_copy(all_ref.at[pl.ds(c * NARROW, NARROW)], held, held_sem)
        load.start()
        if c >= 1:
            seen_copy(c - 1).wait()
        load.wait()

        @pl.loop(0, NARROW)
        def _(f):
            correlate_one(pick_ref, held, made_vis, f)

        seen_copy(c).start()

    def advance(c):
        if 0 <= c - AHEAD < chunks:
            for copy in turn_copies(c - AHEAD)[0]:
                copy.wait_send()
        if c < chunks:
            copies, own = turn_copies(c)
            own.start()
            for copy in copies:
                copy.start()
        if 0 <= c - AHEAD < chunks:
            spread(c - AHEAD)
        if 0 <= c - AHEAD - 1 < chunks:
            hand_on(c - AHEAD - 1)
        if 0 <= c - AHEAD - 2 < chunks:
            products(c - AHEAD - 2)

    for w in range(steps):

        @pl.loop(0, ants // 4)
        def _(q):
            rows = pl.ds(pl.multiple_of(q * 4 * SAMPLES, 4 * SAMPLES), 4 * SAMPLES)
            made = lax.dot_general(
                table_ref[w], filt[rows, :], (((1,), (1,)), ((), ())), preferred_element_type=jnp.float32
            ) * (1.0 / math.sqrt(K))
            for i in range(4):
                for p in range(2):
                    turn[p, pl.ds(q * 4 + i, rows_of, stride=ants), :] = made[
                        p * rows_of : (p + 1) * rows_of, i * SAMPLES : (i + 1) * SAMPLES
                    ]

        @pl.loop(0, rows_of // 8)
        def _(r):
            for p in range(2):
                rows = turn[p, pl.ds(pl.multiple_of(r * 8 * ants, 8 * ants), 8 * ants), :]
                send[w, pl.ds(pl.multiple_of(r * 8, 8), 8), :, p * LANES : (p + 1) * LANES] = rows.reshape(
                    8, ants, LANES
                ).astype(jnp.bfloat16)

        for c in range(w * per, (w + 1) * per):
            advance(c)
    for c in range(chunks, chunks + AHEAD + 2):
        advance(c)
    seen_copy(chunks - 1).wait()
    for c in range(chunks):
        mate_copy(c).wait_send()
        for copy in (*across_copies(c), *passed_copies(c)):
            copy.wait_send()


def correlate_one(pick_ref, held, out_ref, f):
    both = jnp.dot(pick_ref[...], held[f], preferred_element_type=jnp.float32).astype(jnp.bfloat16)
    left, right = both[:PANEL], both[PANEL:]
    turned = jnp.concatenate([-right[:, SAMPLES:], right[:, :SAMPLES]], axis=1)
    for at, other in enumerate((right, turned)):
        summed = lax.dot_general(left, other, (((1,), (1,)), ((), ())), preferred_element_type=jnp.float32)
        out_ref[f, :, at * PANEL : (at + 1) * PANEL] = (summed * (1.0 / SAMPLES)).astype(jnp.bfloat16)


def per_device(groups, tiles, voltages, fir_taps, antenna_order, tile_list):
    ants = voltages.shape[0]
    total = ants * groups * tiles
    channels = K // 2 // groups
    table = jnp.asarray(chunked_table(groups, WIDE))
    steps = channels // WIDE
    chunks = channels // NARROW
    others = max(tiles // 2 - 1, 1)
    dma = pltpu.SemaphoreType.DMA
    tile = tile_list[lax.axis_index("bl")]
    ids = jnp.concatenate(
        [lax.dynamic_slice_in_dim(antenna_order, tile[i] * PANEL, PANEL) for i in range(2)]
    )
    pick = (ids[:, None] == jnp.arange(total, dtype=jnp.int32)[None, :]).astype(jnp.bfloat16)
    seen, _ = pl.pallas_call(
        functools.partial(spectra_kernel, groups, tiles),
        out_shape=(
            jax.ShapeDtypeStruct((channels, PANEL, 2 * PANEL), jnp.bfloat16),
            jax.ShapeDtypeStruct((channels, total, 2 * SAMPLES), jnp.bfloat16),
        ),
        in_specs=[pl.BlockSpec(memory_space=pltpu.VMEM)] * 4,
        out_specs=(pl.BlockSpec(memory_space=pl.ANY),) * 2,
        scratch_shapes=[
            pltpu.VMEM((K // LANES, ants * SAMPLES, LANES), jnp.float32),
            pltpu.VMEM((ants * SAMPLES, K), jnp.bfloat16),
            pltpu.VMEM((2, groups * WIDE * ants, LANES), jnp.float32),
            pltpu.VMEM((steps, groups * WIDE, ants, 2 * SAMPLES), jnp.bfloat16),
            pltpu.VMEM((NARROW, total, 2 * SAMPLES), jnp.bfloat16),
            pltpu.VMEM((NARROW, PANEL, 2 * PANEL), jnp.bfloat16),
            dma, dma,
            dma((chunks,)),
            dma((chunks, groups)), dma((chunks, groups)),
            dma((chunks, others)), dma((chunks, others)),
            dma((chunks,)), dma((chunks,)),
            dma((chunks, others)), dma((chunks, others)),
        ],
        cost_estimate=pl.CostEstimate(flops=10**10, bytes_accessed=10**8, transcendentals=0),
        compiler_params=pltpu.CompilerParams(
            collective_id=0, has_side_effects=True, vmem_limit_bytes=58 * 2**20
        ),
        name="spectra",
    )(voltages, fir_taps, table, pick)
    return seen[None]


def solution(mesh):
    groups, tiles = mesh.shape["freq"], mesh.shape["bl"]

    def run(voltages, fir_taps, antenna_order, tile_list):
        if voltages.shape[0] % 16 == 0 and (K // 2 // groups) % WIDE == 0 and tiles % 2 == 0:
            body = functools.partial(per_device, groups, tiles)
        else:
            body = per_device_plain
        return body(voltages, fir_taps, antenna_order, tile_list)

    return jax.shard_map(
        run,
        mesh=mesh,
        in_specs=(P(("bl", "freq"), None), P(), P(), P()),
        out_specs=P("bl", "freq", None, None),
        check_vma=False,
    )
```

```python
import functools
import math

import jax
import jax.numpy as jnp
import numpy as np
from jax import lax
from jax.experimental import pallas as pl
from jax.experimental.pallas import tpu as pltpu
from jax.sharding import PartitionSpec as P

K = 1024
TAPS = 4
PANEL = 256
SAMPLES = 128
LANES = 128
WIDE = 16
NARROW = 4
AHEAD = 2
MESH = pl.DeviceIdType.MESH


def make_table(points, kept):
    product = (
        jnp.arange(points, dtype=jnp.int32)[:, None]
        * jnp.arange(kept, dtype=jnp.int32)[None, :]
        % points
    )
    phase = 2.0 * math.pi / points * product.astype(jnp.float32)
    return jnp.concatenate([jnp.cos(phase), -jnp.sin(phase)], axis=1).astype(jnp.bfloat16)


def arrange(panel):
    width = panel.shape[1]
    return jnp.transpose(panel, (3, 0, 2, 1)).reshape(panel.shape[3], panel.shape[0], 2 * width)


def rotated(panel):
    turned = jnp.stack([-panel[:, :, 1, :], panel[:, :, 0, :]], axis=2)
    return arrange(turned)


def picked(source, ids):
    pick = (ids[:, None] == jnp.arange(source.shape[0], dtype=jnp.int32)[None, :]).astype(jnp.bfloat16)
    return jnp.einsum("at,tspf->aspf", pick, source, preferred_element_type=jnp.float32).astype(jnp.bfloat16)


def correlate(source, antenna_order, tile):
    row_ids = lax.dynamic_slice_in_dim(antenna_order, tile[0] * PANEL, PANEL)
    col_ids = lax.dynamic_slice_in_dim(antenna_order, tile[1] * PANEL, PANEL)
    row_panel = picked(source, row_ids)
    col_panel = picked(source, col_ids)
    left = arrange(row_panel)
    right = jnp.concatenate([arrange(col_panel), rotated(col_panel)], axis=1)
    return jnp.einsum("fps,fqs->fpq", left, right, preferred_element_type=jnp.float32)


def per_device_plain(voltages, fir_taps, antenna_order, tile_list):
    local_count = voltages.shape[0]
    frames = voltages.reshape(local_count, SAMPLES + TAPS - 1, K)
    filtered = jnp.zeros((local_count, SAMPLES, K), jnp.float32)
    for tap in range(TAPS):
        filtered = filtered + fir_taps[tap][None, None, :] * frames[
            :, tap : tap + SAMPLES, :
        ].astype(jnp.float32)
    filtered = filtered.astype(jnp.bfloat16)
    table = make_table(K, K // 2)
    spectra = jnp.dot(
        filtered.reshape(local_count * SAMPLES, K), table, preferred_element_type=jnp.float32
    )
    spectra = (
        (spectra * (1.0 / math.sqrt(K)))
        .astype(jnp.bfloat16)
        .reshape(local_count, SAMPLES, 2, K // 2)
    )
    turned = lax.all_to_all(spectra, "freq", split_axis=3, concat_axis=0, tiled=True)
    gathered = lax.all_gather(turned, "bl", axis=0, tiled=True)
    own_tile = tile_list[lax.axis_index("bl")]
    summed = correlate(gathered, antenna_order, own_tile)
    return (summed / SAMPLES).astype(jnp.bfloat16)[None]


def chunked_table(groups, width):
    m = np.arange(K)[None, :] * np.arange(K // 2)[:, None] % K
    phase = 2.0 * math.pi / K * m
    table = np.stack([np.cos(phase), -np.sin(phase)])
    table = table.reshape(2, groups, -1, width, K).transpose(2, 0, 1, 3, 4)
    return table.reshape(table.shape[0], 2 * groups * width, K).astype(jnp.bfloat16)


def spectra_kernel(
    groups, tiles, volt_ref, taps_ref, table_ref, pick_ref, seen_ref, all_ref,
    filt32, filt, turn, send, held, made_vis, held_sem, seen_sem, own_sem, s1, r1, s2, r2, s3, r3, s4, r4,
):
    me = lax.axis_index("freq")
    bl = lax.axis_index("bl")
    core = bl % 2
    mate = bl + 1 - 2 * core
    across = [(bl + 2 * e) % tiles for e in range(1, tiles // 2)]
    ants = volt_ref.shape[0]
    block = groups * ants

    barrier = pltpu.get_barrier_semaphore()
    for d in range(1, groups):
        pl.semaphore_signal(barrier, inc=1, device_id={"freq": (me + d) % groups}, device_id_type=MESH)
    for there in (mate, *across):
        pl.semaphore_signal(barrier, inc=1, device_id={"bl": there}, device_id_type=MESH)
    pl.semaphore_wait(barrier, groups - 1 + 1 + len(across))

    @pl.loop(0, SAMPLES // 8)
    def _(step):
        for half in range(K // 256):
            cols = 256 * half
            taps = [taps_ref[t : t + 1, cols : cols + 256] for t in range(TAPS)]
            frames = []
            for i in range(8 + TAPS - 1):
                at = pl.multiple_of((step * 8 + i) * K, K) + cols
                frames.append(volt_ref[:, pl.ds(pl.multiple_of(at, 256), 256)].astype(jnp.float32))
            for i in range(8):
                total = taps[0] * frames[i]
                for t in range(1, TAPS):
                    total = total + taps[t] * frames[i + t]
                for q in range(2):
                    filt32[2 * half + q, pl.ds(step * 8 + i, ants, stride=SAMPLES), :] = total[
                        :, q * LANES : (q + 1) * LANES
                    ]

    @pl.loop(0, ants)
    def _(a):
        rows = pl.ds(pl.multiple_of(a * SAMPLES, SAMPLES), SAMPLES)
        for q in range(K // LANES):
            filt[rows, q * LANES : (q + 1) * LANES] = filt32[q, rows, :].astype(jnp.bfloat16)

    steps = table_ref.shape[0]
    per = WIDE // NARROW
    rows_of = groups * WIDE

    def turn_copies(c):
        h, w = c % per, c // per
        copies = []
        for d in range(1, groups):
            to = (me + d) % groups
            copies.append(
                pltpu.make_async_remote_copy(
                    src_ref=send.at[w, pl.ds(to * WIDE + h * NARROW, NARROW)],
                    dst_ref=all_ref.at[
                        pl.ds(c * NARROW, NARROW), pl.ds(pl.multiple_of(bl * block + me * ants, ants), ants)
                    ],
                    send_sem=s1.at[c, d],
                    recv_sem=r1.at[c, d],
                    device_id={"freq": to},
                    device_id_type=MESH,
                )
            )
        own = pltpu.make_async_copy(
            send.at[w, pl.ds(me * WIDE + h * NARROW, NARROW)],
            all_ref.at[pl.ds(c * NARROW, NARROW), pl.ds(pl.multiple_of(bl * block + me * ants, ants), ants)],
            own_sem.at[c],
        )
        return copies, own

    def block_of(c, b):
        return all_ref.at[pl.ds(c * NARROW, NARROW), pl.ds(pl.multiple_of(b * block, block), block)]

    def block_copy(c, b, there, ssem, rsem):
        return pltpu.make_async_remote_copy(
            src_ref=block_of(c, b), dst_ref=block_of(c, b), send_sem=ssem, recv_sem=rsem,
            device_id={"bl": there}, device_id_type=MESH,
        )

    def across_copies(c):
        return [block_copy(c, bl, there, s2.at[c, e], r2.at[c, e]) for e, there in enumerate(across)]

    def mate_copy(c):
        return block_copy(c, bl, mate, s3.at[c], r3.at[c])

    def passed_copies(c):
        return [
            block_copy(c, (bl + tiles - 2 * (e + 1)) % tiles, mate, s4.at[c, e], r4.at[c, e])
            for e in range(len(across))
        ]

    chunks = steps * per

    def spread(c):
        copies, own = turn_copies(c)
        for copy in copies:
            copy.wait_recv()
        own.wait()
        for copy in across_copies(c):
            copy.start()
        mate_copy(c).start()

    def hand_on(c):
        arrived, passed = across_copies(c), passed_copies(c)
        for one, two in zip(arrived, passed):
            one.wait_recv()
            two.start()

    def seen_copy(c):
        return pltpu.make_async_copy(made_vis, seen_ref.at[pl.ds(c * NARROW, NARROW)], seen_sem)

    def products(c):
        mate_copy(c).wait_recv()
        for copy in passed_copies(c):
            copy.wait_recv()
        load = pltpu.make_async_copy(all_ref.at[pl.ds(c * NARROW, NARROW)], held, held_sem)
        load.start()
        if c >= 1:
            seen_copy(c - 1).wait()
        load.wait()

        @pl.loop(0, NARROW)
        def _(f):
            correlate_one(pick_ref, held, made_vis, f)

        seen_copy(c).start()

    def advance(c):
        sent = 0 if c == 1 else c - AHEAD
        if (sent > 0 or c == 1) and sent < chunks:
            for copy in turn_copies(sent)[0]:
                copy.wait_send()
        if c < chunks:
            copies, own = turn_copies(c)
            own.start()
            for copy in copies:
                copy.start()
        if 0 <= c - AHEAD < chunks:
            spread(c - AHEAD)
        if 0 <= c - AHEAD - 1 < chunks:
            hand_on(c - AHEAD - 1)
        if 0 <= c - AHEAD - 2 < chunks:
            products(c - AHEAD - 2)

    for w in range(steps):

        @pl.loop(0, ants // 4)
        def _(q):
            rows = pl.ds(pl.multiple_of(q * 4 * SAMPLES, 4 * SAMPLES), 4 * SAMPLES)
            made = lax.dot_general(
                table_ref[w], filt[rows, :], (((1,), (1,)), ((), ())), preferred_element_type=jnp.float32
            ) * (1.0 / math.sqrt(K))
            for i in range(4):
                for p in range(2):
                    turn[p, pl.ds(q * 4 + i, rows_of, stride=ants), :] = made[
                        p * rows_of : (p + 1) * rows_of, i * SAMPLES : (i + 1) * SAMPLES
                    ]

        @pl.loop(0, rows_of // 8)
        def _(r):
            for p in range(2):
                rows = turn[p, pl.ds(pl.multiple_of(r * 8 * ants, 8 * ants), 8 * ants), :]
                send[w, pl.ds(pl.multiple_of(r * 8, 8), 8), :, p * LANES : (p + 1) * LANES] = rows.reshape(
                    8, ants, LANES
                ).astype(jnp.bfloat16)

        for c in range(w * per, (w + 1) * per):
            advance(c)
    for c in range(chunks, chunks + AHEAD + 2):
        advance(c)
    seen_copy(chunks - 1).wait()
    for c in range(chunks):
        mate_copy(c).wait_send()
        for copy in (*across_copies(c), *passed_copies(c)):
            copy.wait_send()


def correlate_one(pick_ref, held, out_ref, f):
    both = jnp.dot(pick_ref[...], held[f], preferred_element_type=jnp.float32).astype(jnp.bfloat16)
    left, right = both[:PANEL], both[PANEL:]
    turned = jnp.concatenate([-right[:, SAMPLES:], right[:, :SAMPLES]], axis=1)
    for at, other in enumerate((right, turned)):
        summed = lax.dot_general(left, other, (((1,), (1,)), ((), ())), preferred_element_type=jnp.float32)
        out_ref[f, :, at * PANEL : (at + 1) * PANEL] = (summed * (1.0 / SAMPLES)).astype(jnp.bfloat16)


def per_device(groups, tiles, voltages, fir_taps, antenna_order, tile_list):
    ants = voltages.shape[0]
    total = ants * groups * tiles
    channels = K // 2 // groups
    table = jnp.asarray(chunked_table(groups, WIDE))
    steps = channels // WIDE
    chunks = channels // NARROW
    others = max(tiles // 2 - 1, 1)
    dma = pltpu.SemaphoreType.DMA
    tile = tile_list[lax.axis_index("bl")]
    ids = jnp.concatenate(
        [lax.dynamic_slice_in_dim(antenna_order, tile[i] * PANEL, PANEL) for i in range(2)]
    )
    pick = (ids[:, None] == jnp.arange(total, dtype=jnp.int32)[None, :]).astype(jnp.bfloat16)
    seen, _ = pl.pallas_call(
        functools.partial(spectra_kernel, groups, tiles),
        out_shape=(
            jax.ShapeDtypeStruct((channels, PANEL, 2 * PANEL), jnp.bfloat16),
            jax.ShapeDtypeStruct((channels, total, 2 * SAMPLES), jnp.bfloat16),
        ),
        in_specs=[pl.BlockSpec(memory_space=pltpu.VMEM)] * 4,
        out_specs=(pl.BlockSpec(memory_space=pl.ANY),) * 2,
        scratch_shapes=[
            pltpu.VMEM((K // LANES, ants * SAMPLES, LANES), jnp.float32),
            pltpu.VMEM((ants * SAMPLES, K), jnp.bfloat16),
            pltpu.VMEM((2, groups * WIDE * ants, LANES), jnp.float32),
            pltpu.VMEM((steps, groups * WIDE, ants, 2 * SAMPLES), jnp.bfloat16),
            pltpu.VMEM((NARROW, total, 2 * SAMPLES), jnp.bfloat16),
            pltpu.VMEM((NARROW, PANEL, 2 * PANEL), jnp.bfloat16),
            dma, dma,
            dma((chunks,)),
            dma((chunks, groups)), dma((chunks, groups)),
            dma((chunks, others)), dma((chunks, others)),
            dma((chunks,)), dma((chunks,)),
            dma((chunks, others)), dma((chunks, others)),
        ],
        cost_estimate=pl.CostEstimate(flops=10**10, bytes_accessed=10**8, transcendentals=0),
        compiler_params=pltpu.CompilerParams(
            collective_id=0, has_side_effects=True, vmem_limit_bytes=58 * 2**20
        ),
        name="spectra",
    )(voltages, fir_taps, table, pick)
    return seen[None]


def solution(mesh):
    groups, tiles = mesh.shape["freq"], mesh.shape["bl"]

    def run(voltages, fir_taps, antenna_order, tile_list):
        if voltages.shape[0] % 16 == 0 and (K // 2 // groups) % WIDE == 0 and tiles % 2 == 0:
            body = functools.partial(per_device, groups, tiles)
        else:
            body = per_device_plain
        return body(voltages, fir_taps, antenna_order, tile_list)

    return jax.shard_map(
        run,
        mesh=mesh,
        in_specs=(P(("bl", "freq"), None), P(), P(), P()),
        out_specs=P("bl", "freq", None, None),
        check_vma=False,
    )
```

```python
import functools
import math

import jax
import jax.numpy as jnp
import numpy as np
from jax import lax
from jax.experimental import pallas as pl
from jax.experimental.pallas import tpu as pltpu
from jax.sharding import PartitionSpec as P

K = 1024
TAPS = 4
PANEL = 256
SAMPLES = 128
LANES = 128
WIDE = 8
NARROW = 4
AHEAD = 2
MESH = pl.DeviceIdType.MESH


def make_table(points, kept):
    product = (
        jnp.arange(points, dtype=jnp.int32)[:, None]
        * jnp.arange(kept, dtype=jnp.int32)[None, :]
        % points
    )
    phase = 2.0 * math.pi / points * product.astype(jnp.float32)
    return jnp.concatenate([jnp.cos(phase), -jnp.sin(phase)], axis=1).astype(jnp.bfloat16)


def arrange(panel):
    width = panel.shape[1]
    return jnp.transpose(panel, (3, 0, 2, 1)).reshape(panel.shape[3], panel.shape[0], 2 * width)


def rotated(panel):
    turned = jnp.stack([-panel[:, :, 1, :], panel[:, :, 0, :]], axis=2)
    return arrange(turned)


def picked(source, ids):
    pick = (ids[:, None] == jnp.arange(source.shape[0], dtype=jnp.int32)[None, :]).astype(jnp.bfloat16)
    return jnp.einsum("at,tspf->aspf", pick, source, preferred_element_type=jnp.float32).astype(jnp.bfloat16)


def correlate(source, antenna_order, tile):
    row_ids = lax.dynamic_slice_in_dim(antenna_order, tile[0] * PANEL, PANEL)
    col_ids = lax.dynamic_slice_in_dim(antenna_order, tile[1] * PANEL, PANEL)
    row_panel = picked(source, row_ids)
    col_panel = picked(source, col_ids)
    left = arrange(row_panel)
    right = jnp.concatenate([arrange(col_panel), rotated(col_panel)], axis=1)
    return jnp.einsum("fps,fqs->fpq", left, right, preferred_element_type=jnp.float32)


def per_device_plain(voltages, fir_taps, antenna_order, tile_list):
    local_count = voltages.shape[0]
    frames = voltages.reshape(local_count, SAMPLES + TAPS - 1, K)
    filtered = jnp.zeros((local_count, SAMPLES, K), jnp.float32)
    for tap in range(TAPS):
        filtered = filtered + fir_taps[tap][None, None, :] * frames[
            :, tap : tap + SAMPLES, :
        ].astype(jnp.float32)
    filtered = filtered.astype(jnp.bfloat16)
    table = make_table(K, K // 2)
    spectra = jnp.dot(
        filtered.reshape(local_count * SAMPLES, K), table, preferred_element_type=jnp.float32
    )
    spectra = (
        (spectra * (1.0 / math.sqrt(K)))
        .astype(jnp.bfloat16)
        .reshape(local_count, SAMPLES, 2, K // 2)
    )
    turned = lax.all_to_all(spectra, "freq", split_axis=3, concat_axis=0, tiled=True)
    gathered = lax.all_gather(turned, "bl", axis=0, tiled=True)
    own_tile = tile_list[lax.axis_index("bl")]
    summed = correlate(gathered, antenna_order, own_tile)
    return (summed / SAMPLES).astype(jnp.bfloat16)[None]


def chunked_table(groups, width):
    m = np.arange(K)[None, :] * np.arange(K // 2)[:, None] % K
    phase = 2.0 * math.pi / K * m
    table = np.stack([np.cos(phase), -np.sin(phase)])
    table = table.reshape(2, groups, -1, width, K).transpose(2, 0, 1, 3, 4)
    return table.reshape(table.shape[0], 2 * groups * width, K).astype(jnp.bfloat16)


def spectra_kernel(
    groups, tiles, volt_ref, taps_ref, table_ref, pick_ref, seen_ref, all_ref,
    filt32, filt, turn, send, held, made_vis, held_sem, seen_sem, own_sem, s1, r1, s2, r2, s3, r3, s4, r4,
):
    me = lax.axis_index("freq")
    bl = lax.axis_index("bl")
    core = bl % 2
    mate = bl + 1 - 2 * core
    across = [(bl + 2 * e) % tiles for e in range(1, tiles // 2)]
    ants = volt_ref.shape[0]
    block = groups * ants

    barrier = pltpu.get_barrier_semaphore()
    for d in range(1, groups):
        pl.semaphore_signal(barrier, inc=1, device_id={"freq": (me + d) % groups}, device_id_type=MESH)
    for there in (mate, *across):
        pl.semaphore_signal(barrier, inc=1, device_id={"bl": there}, device_id_type=MESH)
    pl.semaphore_wait(barrier, groups - 1 + 1 + len(across))

    @pl.loop(0, SAMPLES // 8)
    def _(step):
        for half in range(K // 256):
            cols = 256 * half
            taps = [taps_ref[t : t + 1, cols : cols + 256] for t in range(TAPS)]
            frames = []
            for i in range(8 + TAPS - 1):
                at = pl.multiple_of((step * 8 + i) * K, K) + cols
                frames.append(volt_ref[:, pl.ds(pl.multiple_of(at, 256), 256)].astype(jnp.float32))
            for i in range(8):
                total = taps[0] * frames[i]
                for t in range(1, TAPS):
                    total = total + taps[t] * frames[i + t]
                for q in range(2):
                    filt32[2 * half + q, pl.ds(step * 8 + i, ants, stride=SAMPLES), :] = total[
                        :, q * LANES : (q + 1) * LANES
                    ]

    @pl.loop(0, ants)
    def _(a):
        rows = pl.ds(pl.multiple_of(a * SAMPLES, SAMPLES), SAMPLES)
        for q in range(K // LANES):
            filt[rows, q * LANES : (q + 1) * LANES] = filt32[q, rows, :].astype(jnp.bfloat16)

    steps = table_ref.shape[0]
    per = WIDE // NARROW
    rows_of = groups * WIDE

    def turn_copies(c):
        h, w = c % per, c // per
        copies = []
        for d in range(1, groups):
            to = (me + d) % groups
            copies.append(
                pltpu.make_async_remote_copy(
                    src_ref=send.at[w, pl.ds(to * WIDE + h * NARROW, NARROW)],
                    dst_ref=all_ref.at[
                        pl.ds(c * NARROW, NARROW), pl.ds(pl.multiple_of(bl * block + me * ants, ants), ants)
                    ],
                    send_sem=s1.at[c, d],
                    recv_sem=r1.at[c, d],
                    device_id={"freq": to},
                    device_id_type=MESH,
                )
            )
        own = pltpu.make_async_copy(
            send.at[w, pl.ds(me * WIDE + h * NARROW, NARROW)],
            all_ref.at[pl.ds(c * NARROW, NARROW), pl.ds(pl.multiple_of(bl * block + me * ants, ants), ants)],
            own_sem.at[c],
        )
        return copies, own

    def block_of(c, b):
        return all_ref.at[pl.ds(c * NARROW, NARROW), pl.ds(pl.multiple_of(b * block, block), block)]

    def block_copy(c, b, there, ssem, rsem):
        return pltpu.make_async_remote_copy(
            src_ref=block_of(c, b), dst_ref=block_of(c, b), send_sem=ssem, recv_sem=rsem,
            device_id={"bl": there}, device_id_type=MESH,
        )

    def across_copies(c):
        return [block_copy(c, bl, there, s2.at[c, e], r2.at[c, e]) for e, there in enumerate(across)]

    def mate_copy(c):
        return block_copy(c, bl, mate, s3.at[c], r3.at[c])

    def passed_copies(c):
        return [
            block_copy(c, (bl + tiles - 2 * (e + 1)) % tiles, mate, s4.at[c, e], r4.at[c, e])
            for e in range(len(across))
        ]

    chunks = steps * per

    def spread(c):
        copies, own = turn_copies(c)
        for copy in copies:
            copy.wait_recv()
        own.wait()
        for copy in across_copies(c):
            copy.start()
        mate_copy(c).start()

    def hand_on(c):
        arrived, passed = across_copies(c), passed_copies(c)
        for one, two in zip(arrived, passed):
            one.wait_recv()
            two.start()

    def seen_copy(c):
        return pltpu.make_async_copy(made_vis, seen_ref.at[pl.ds(c * NARROW, NARROW)], seen_sem)

    def products(c):
        mate_copy(c).wait_recv()
        for copy in passed_copies(c):
            copy.wait_recv()
        load = pltpu.make_async_copy(all_ref.at[pl.ds(c * NARROW, NARROW)], held, held_sem)
        load.start()
        if c >= 1:
            seen_copy(c - 1).wait()
        load.wait()

        @pl.loop(0, NARROW)
        def _(f):
            correlate_one(pick_ref, held, made_vis, f)

        seen_copy(c).start()

    def advance(c):
        sent = 0 if c == 1 else c - AHEAD
        if (sent > 0 or c == 1) and sent < chunks:
            for copy in turn_copies(sent)[0]:
                copy.wait_send()
        if c < chunks:
            copies, own = turn_copies(c)
            own.start()
            for copy in copies:
                copy.start()
        if 0 <= c - AHEAD < chunks:
            spread(c - AHEAD)
        if 0 <= c - AHEAD - 1 < chunks:
            hand_on(c - AHEAD - 1)
        if 0 <= c - AHEAD - 2 < chunks:
            products(c - AHEAD - 2)

    for w in range(steps):

        @pl.loop(0, ants // 4)
        def _(q):
            rows = pl.ds(pl.multiple_of(q * 4 * SAMPLES, 4 * SAMPLES), 4 * SAMPLES)
            made = lax.dot_general(
                table_ref[w], filt[rows, :], (((1,), (1,)), ((), ())), preferred_element_type=jnp.float32
            ) * (1.0 / math.sqrt(K))
            for i in range(4):
                for p in range(2):
                    turn[p, pl.ds(q * 4 + i, rows_of, stride=ants), :] = made[
                        p * rows_of : (p + 1) * rows_of, i * SAMPLES : (i + 1) * SAMPLES
                    ]

        @pl.loop(0, rows_of // 8)
        def _(r):
            for p in range(2):
                rows = turn[p, pl.ds(pl.multiple_of(r * 8 * ants, 8 * ants), 8 * ants), :]
                send[w, pl.ds(pl.multiple_of(r * 8, 8), 8), :, p * LANES : (p + 1) * LANES] = rows.reshape(
                    8, ants, LANES
                ).astype(jnp.bfloat16)

        for c in range(w * per, (w + 1) * per):
            advance(c)
    for c in range(chunks, chunks + AHEAD + 2):
        advance(c)
    seen_copy(chunks - 1).wait()
    for c in range(chunks):
        mate_copy(c).wait_send()
        for copy in (*across_copies(c), *passed_copies(c)):
            copy.wait_send()


def correlate_one(pick_ref, held, out_ref, f):
    both = jnp.dot(pick_ref[...], held[f], preferred_element_type=jnp.float32).astype(jnp.bfloat16)
    left, right = both[:PANEL], both[PANEL:]
    turned = jnp.concatenate([-right[:, SAMPLES:], right[:, :SAMPLES]], axis=1)
    for at, other in enumerate((right, turned)):
        summed = lax.dot_general(left, other, (((1,), (1,)), ((), ())), preferred_element_type=jnp.float32)
        out_ref[f, :, at * PANEL : (at + 1) * PANEL] = (summed * (1.0 / SAMPLES)).astype(jnp.bfloat16)


def per_device(groups, tiles, voltages, fir_taps, antenna_order, tile_list):
    ants = voltages.shape[0]
    total = ants * groups * tiles
    channels = K // 2 // groups
    table = jnp.asarray(chunked_table(groups, WIDE))
    steps = channels // WIDE
    chunks = channels // NARROW
    others = max(tiles // 2 - 1, 1)
    dma = pltpu.SemaphoreType.DMA
    tile = tile_list[lax.axis_index("bl")]
    ids = jnp.concatenate(
        [lax.dynamic_slice_in_dim(antenna_order, tile[i] * PANEL, PANEL) for i in range(2)]
    )
    pick = (ids[:, None] == jnp.arange(total, dtype=jnp.int32)[None, :]).astype(jnp.bfloat16)
    seen, _ = pl.pallas_call(
        functools.partial(spectra_kernel, groups, tiles),
        out_shape=(
            jax.ShapeDtypeStruct((channels, PANEL, 2 * PANEL), jnp.bfloat16),
            jax.ShapeDtypeStruct((channels, total, 2 * SAMPLES), jnp.bfloat16),
        ),
        in_specs=[pl.BlockSpec(memory_space=pltpu.VMEM)] * 4,
        out_specs=(pl.BlockSpec(memory_space=pl.ANY),) * 2,
        scratch_shapes=[
            pltpu.VMEM((K // LANES, ants * SAMPLES, LANES), jnp.float32),
            pltpu.VMEM((ants * SAMPLES, K), jnp.bfloat16),
            pltpu.VMEM((2, groups * WIDE * ants, LANES), jnp.float32),
            pltpu.VMEM((steps, groups * WIDE, ants, 2 * SAMPLES), jnp.bfloat16),
            pltpu.VMEM((NARROW, total, 2 * SAMPLES), jnp.bfloat16),
            pltpu.VMEM((NARROW, PANEL, 2 * PANEL), jnp.bfloat16),
            dma, dma,
            dma((chunks,)),
            dma((chunks, groups)), dma((chunks, groups)),
            dma((chunks, others)), dma((chunks, others)),
            dma((chunks,)), dma((chunks,)),
            dma((chunks, others)), dma((chunks, others)),
        ],
        cost_estimate=pl.CostEstimate(flops=10**10, bytes_accessed=10**8, transcendentals=0),
        compiler_params=pltpu.CompilerParams(
            collective_id=0, has_side_effects=True, vmem_limit_bytes=58 * 2**20
        ),
        name="spectra",
    )(voltages, fir_taps, table, pick)
    return seen[None]


def solution(mesh):
    groups, tiles = mesh.shape["freq"], mesh.shape["bl"]

    def run(voltages, fir_taps, antenna_order, tile_list):
        if voltages.shape[0] % 16 == 0 and (K // 2 // groups) % WIDE == 0 and tiles % 2 == 0:
            body = functools.partial(per_device, groups, tiles)
        else:
            body = per_device_plain
        return body(voltages, fir_taps, antenna_order, tile_list)

    return jax.shard_map(
        run,
        mesh=mesh,
        in_specs=(P(("bl", "freq"), None), P(), P(), P()),
        out_specs=P("bl", "freq", None, None),
        check_vma=False,
    )
```
